512 devices in a mesh: section: 16 (over y, x_lo), expert: 16 (over z, x_hi), tensor: 2 (over core).
Axes of the slice: x: 4 (x_hi: 2, x_lo: 2; x = x_hi * 2 + x_lo), y: 8, z: 8, core: 2. Of those that a mesh axis runs over, the one named last changes fastest.
Arguments:
- activations: bfloat16 [16, 2048, 2560], P('section', 'expert', 'tensor'), may hold values from -6 to 6
- norm_gain: bfloat16 [16, 2560], P('section'), may hold values from 0.099609375 to 1.8984375
- w_gate: bfloat16 [16, 2560, 8192], P('section', None, ('expert', 'tensor')), may hold values from -0.125 to 0.125
- w_up: bfloat16 [16, 2560, 8192], P('section', None, ('expert', 'tensor')), may hold values from -0.125 to 0.125
- w_down: bfloat16 [16, 8192, 2560], P('section', ('expert', 'tensor')), may hold values from -0.1875 to 0.1875
- route_ids: int32 [2, 16, 2048, 6], P(None, 'section', 'expert'), may hold values from 0 to 159, all different within a row; in each aligned block of 128 rows (0 to 127, 128 to 255, ..., all dimensions but the last counted through in order) at most 8 rows name the same one
- route_weights: float32 [2, 16, 2048, 6], P(None, 'section', 'expert'), may hold values from 0.25 to 2.5
Outputs:
- advanced: bfloat16 [16, 2048, 2560], P('section', 'expert', 'tensor')
The draws below stay inside these ranges and needn't reach their ends.
Inputs may be any that keep to these rules, and one draw needn't show every extreme that they name: `route_ids`: each row names 6 different experts. Within the rows of one device (aligned blocks of 128 rows, for each tick and section) no expert is named by more than 8 rows, and in some blocks one expert is named by exactly 8.
All inputs are finite; a program needn't handle non-finite values.
Results may differ from the reference program's by a relative error of at most 0.01.
Values may be sent and summed in bfloat16 or wider, within the bound.
No kernel may reach another device: no remote copies, remote signals or barrier semaphores. Data moves between devices by JAX's collectives and lax.ppermute only.
A program may use at most 64 MiB of HBM per device.

```python
import math
import jax
import jax.numpy as jnp
import numpy as np
from jax import lax

D = 2560
H_EXP = 1024
EXP_ALL = 160
TOP = 6
TICKS = 2
TOK_DEV = 128
CAP = 8
WIN = 8
COLS = 8192
SECTIONS = 16
TOKENS = 2048
N_EXPERT = 16


def block_scale(stream_key, shape, shards, low, high):
    level = 1.0
    for axis_at, blocks in shards:
        heights = jax.random.uniform(jax.random.fold_in(jax.random.fold_in(stream_key, 6), axis_at), (blocks,), jnp.float32, low / len(shards), high / len(shards))
        level = level * jnp.repeat(jnp.exp(heights), shape[axis_at] // blocks).reshape((-1,) + (1,) * (len(shape) - 1 - axis_at))
    return level


def deal_out(rng, own, number, rows, count, top, most, skew):
    sequence = jax.random.permutation(rng, count)
    crowded, usual = shares(count, rows * top, most, skew, True), shares(count, rows * top, most, skew, False)
    places = jnp.arange(count)

    def named(sizes, turn):
        used = int((sizes > 0).sum())
        fixed = max(1, used // 4)
        passed = fixed + (places - fixed + turn * (used - fixed)) % max(1, count - fixed)
        return jnp.zeros((count,), jnp.int32).at[sequence[jnp.where(places < fixed, places, passed)]].set(jnp.asarray(sizes, jnp.int32))

    sizes = jnp.where(number % 4 == 0, named(crowded, number // 4), named(usual, number - number // 4 - 1))
    mixed = jax.random.permutation(jax.random.fold_in(own, 3), count)
    donor, taker = mixed[0:count // 2 * 2:2], mixed[1:count // 2 * 2:2]
    slack = jnp.minimum(sizes[donor] - 1, most - sizes[taker]) // 2
    slack = jnp.where((donor == sequence[0]) | (taker == sequence[0]) | (sizes[taker] == 0), 0, jnp.maximum(slack, 0))
    passed = jax.random.randint(jax.random.fold_in(own, 4), (count // 2,), 0, 1 << 20) % (slack + 1)
    sizes = sizes.at[donor].add(-passed).at[taker].add(passed)
    labels = jnp.searchsorted(jnp.cumsum(sizes), jnp.arange(rows * top), side="right").astype(jnp.int32)
    grid = labels.reshape(top, rows).T
    grid = grid[jax.random.permutation(jax.random.fold_in(own, 1), rows)]
    turn = jax.random.randint(jax.random.fold_in(own, 2), (rows, 1), 0, top)
    return jnp.take_along_axis(grid, (jnp.arange(top)[None, :] + turn) % top, axis=1)


def shares(count, total, most, skew, full):
    loads = [(1 << 20) // math.isqrt(grade ** skew) + 1 for grade in range(1, count + 1)]
    largest = most if full else min(most, max(-(-total // count), total * loads[0] // sum(loads)))
    least = 1 if total - largest >= count - 1 else 0
    holding, surplus = [largest] + [least] * (count - 1), total - largest - least * (count - 1)
    while surplus > 0:
        movable = [i for i in range(1, count) if holding[i] < largest] or [i for i in range(1, count) if holding[i] < most]
        pool, remaining = sum([loads[i] for i in movable]), surplus
        for i in movable:
            addition = min(most - holding[i], max(1, remaining * loads[i] // pool), surplus)
            holding[i] = holding[i] + addition
            surplus = surplus - addition
    return np.array(holding)


def noise(rng, extent, deviation, reach, pieces=(), kind=jnp.bfloat16):
    values = deviation * jax.random.normal(rng, extent, jnp.float32)
    if pieces:
        values = values * block_scale(rng, extent, pieces, -0.22, 0.18)
    return jnp.clip(values, -reach, reach).astype(kind)


def setup_inputs(seed: int = 0) -> dict:
    splits = jax.random.split(jax.random.key(seed), 8)
    activations = noise(splits[0], (SECTIONS, TOKENS, D), 1.0, 6.0, ((0, 16), (1, 16), (2, 2)))
    norm_gain = jnp.clip(1.0 + 0.18 * jax.random.normal(splits[1], (SECTIONS, D), jnp.float32), 0.099609375, 1.8984375).astype(jnp.bfloat16)
    w_gate = noise(splits[2], (SECTIONS, D, COLS), D ** -0.5, 0.125, ((0, 16), (2, 32)))
    w_up = noise(splits[3], (SECTIONS, D, COLS), D ** -0.5, 0.125, ((0, 16), (2, 32)))
    w_down = noise(splits[4], (SECTIONS, COLS, D), H_EXP ** -0.5, 0.1875, ((0, 16), (1, 32)))
    route_ids_keys = jax.random.split(jax.random.fold_in(splits[5], 1), TICKS * SECTIONS * TOKENS // TOK_DEV)
    route_ids_turns = jax.random.permutation(jax.random.fold_in(splits[5], 3), TICKS * SECTIONS * TOKENS // TOK_DEV)
    route_ids = jax.vmap(lambda own, number: deal_out(jax.random.fold_in(splits[5], 2), own, number, TOK_DEV, EXP_ALL, TOP, CAP, 2))(route_ids_keys, route_ids_turns).reshape((TICKS, SECTIONS, TOKENS, TOP))
    route_weights = jnp.clip(jnp.exp(math.log(2.5) - 2.3025851 * jax.random.uniform(splits[6], (TICKS, SECTIONS, TOKENS, TOP), jnp.float32) ** block_scale(splits[6], (TICKS, SECTIONS, TOKENS, TOP), ((1, 16), (2, 16)), -0.2, 0.2)), 0.25, 2.5)
    return {"activations": activations, "norm_gain": norm_gain, "w_gate": w_gate, "w_up": w_up, "w_down": w_down, "route_ids": route_ids, "route_weights": route_weights}


NORM_EPS = 1e-06

def slot_tables(block_ids):
    tok_count = block_ids.shape[0]
    entries = block_ids.reshape(-1)
    inside = entries < WIN
    experts_row = jnp.arange(WIN, dtype=jnp.int32)
    onehot = (entries[:, None] == experts_row[None, :]).astype(jnp.int32)
    earlier = jnp.cumsum(onehot, axis=0, dtype=jnp.int32) - onehot
    slot_of = lax.optimization_barrier(jnp.sum(earlier * onehot, axis=1, dtype=jnp.int32))
    position = jnp.where(inside, entries * CAP + slot_of, WIN * CAP).astype(jnp.int32)
    owners = jnp.full((WIN * CAP,), tok_count, jnp.int32)
    sources = jnp.arange(tok_count * TOP, dtype=jnp.int32) // TOP
    owners = owners.at[position].set(sources, mode='drop')
    return (position, owners)

def take_rows(source_rows, row_index):
    return source_rows[row_index]

def section_layer(packed):
    current, gain_row, gate_w, up_w, down_w, ids_now, weights_now = packed
    block_count = N_EXPERT
    as_float = current.astype(jnp.float32)
    rms_scale = jnp.sqrt(lax.optimization_barrier(jnp.mean(as_float * as_float, axis=1, keepdims=True)) + NORM_EPS)
    normed = (as_float / rms_scale * gain_row.astype(jnp.float32)).astype(jnp.bfloat16)
    position, owners = jax.vmap(slot_tables)(ids_now.reshape(block_count, TOK_DEV, TOP))
    padded = jnp.concatenate([normed.reshape(block_count, TOK_DEV, D), jnp.zeros((block_count, 1, D), jnp.bfloat16)], axis=1)
    gathered = jax.vmap(take_rows)(padded, owners)
    by_expert = gathered.reshape(block_count, WIN, CAP, D).transpose(1, 0, 2, 3).reshape(WIN, block_count * CAP, D)
    quarter_width = H_EXP // 4

    def run_expert(bundle):
        expert_index, slot_rows = bundle
        running = jnp.zeros((block_count * CAP, D), jnp.float32)
        for quarter_index in range(4):
            column_start = (expert_index * H_EXP + quarter_index * quarter_width).astype(jnp.int32)
            gate_cols = lax.dynamic_slice_in_dim(gate_w, column_start, quarter_width, 1)
            up_cols = lax.dynamic_slice_in_dim(up_w, column_start, quarter_width, 1)
            down_rows = lax.dynamic_slice_in_dim(down_w, column_start, quarter_width, 0)
            gate_act = jnp.dot(slot_rows, gate_cols, preferred_element_type=jnp.float32)
            up_act = jnp.dot(slot_rows, up_cols, preferred_element_type=jnp.float32)
            hidden = (jax.nn.silu(gate_act) * up_act).astype(jnp.bfloat16)
            part_q = jnp.dot(hidden, down_rows, preferred_element_type=jnp.float32).astype(jnp.bfloat16)
            running = running + lax.optimization_barrier(part_q).astype(jnp.float32)
        return running
    outputs = lax.map(run_expert, (jnp.arange(WIN, dtype=jnp.int32), by_expert))
    per_block = outputs.reshape(WIN, block_count, CAP, D).transpose(1, 0, 2, 3).reshape(block_count, WIN * CAP, D)
    padded_out = jnp.concatenate([per_block, jnp.zeros((block_count, 1, D), jnp.float32)], axis=1)
    picked_slots = position.reshape(block_count, TOK_DEV, TOP)
    weights_block = weights_now.reshape(block_count, TOK_DEV, TOP)
    moe_sum = jnp.zeros((block_count, TOK_DEV, D), jnp.float32)
    for pick_index in range(TOP):
        picked = jax.vmap(take_rows)(padded_out, picked_slots[:, :, pick_index])
        moe_sum = moe_sum + picked * weights_block[:, :, pick_index, None]
    return (as_float + moe_sum.reshape(TOKENS, D)).astype(jnp.bfloat16)

def reference(activations, norm_gain, w_gate, w_up, w_down, route_ids, route_weights):
    current = activations
    for tick_index in range(TICKS):
        current = jnp.roll(current, 1, axis=0)
        current = lax.map(section_layer, (current, norm_gain, w_gate, w_up, w_down, route_ids[tick_index], route_weights[tick_index]))
    return current
```

```python
import jax
import jax.numpy as jnp
from jax import lax
from jax.sharding import PartitionSpec as P

TICKS = 2


NORM_EPS = 1e-06


def from_behind(array, axis, by):
    devices = lax.axis_size(axis)
    return lax.ppermute(array, axis, [(i, (i + by) % devices) for i in range(devices)])


def route_tables(block_ids, block_weights, window, capacity):
    tok_count = block_ids.shape[0]
    ids_major = block_ids.T
    weights_major = block_weights.T
    experts_col = jnp.arange(window, dtype=jnp.int32)[None, :, None]
    member = ids_major[:, None, :] == experts_col
    named = jnp.sum(member.astype(jnp.float32), axis=0)
    gate_of = jnp.sum(jnp.where(member, weights_major[:, None, :], 0.0), axis=0)
    row_pos = jnp.arange(tok_count, dtype=jnp.int32)
    strictly = (row_pos[:, None] < row_pos[None, :]).astype(jnp.bfloat16)
    earlier = jnp.dot(named.astype(jnp.bfloat16), strictly, preferred_element_type=jnp.float32)
    slot_col = jnp.arange(capacity, dtype=jnp.float32)[None, :, None]
    filled = named[:, None, :] * (earlier[:, None, :] == slot_col).astype(jnp.float32)
    dispatch_table = filled.reshape(window * capacity, tok_count)
    combine_table = (filled * gate_of[:, None, :]).reshape(window * capacity, tok_count)
    return (dispatch_table.astype(jnp.bfloat16), combine_table)


def local(activations, norm_gain, w_gate, w_up, w_down, route_ids, route_weights):
    current = activations[0]
    tok_rows = current.shape[0]
    half_width = current.shape[1]
    full_width = half_width * lax.axis_size("tensor")
    expert_count = lax.axis_size("expert")
    window = expert_count // 2
    capacity = tok_rows // 16
    gain_row = norm_gain[0].astype(jnp.float32)
    gate_w = w_gate[0]
    up_w = w_up[0]
    down_w = lax.all_to_all(w_down[0], "tensor", split_axis=1, concat_axis=0, tiled=True)
    for tick_index in range(TICKS):
        current = from_behind(current, "section", 1)
        dispatch_table, combine_table = route_tables(
            route_ids[tick_index, 0], route_weights[tick_index, 0], window, capacity
        )
        dispatch_twice = jnp.repeat(
            dispatch_table.reshape(window, capacity, tok_rows), 2, axis=0
        ).reshape(expert_count * capacity, tok_rows)
        outgoing = jnp.dot(dispatch_twice, current, preferred_element_type=jnp.float32).astype(
            jnp.bfloat16
        )
        arrived = lax.all_to_all(
            outgoing.reshape(expert_count, capacity, half_width),
            "expert",
            split_axis=0,
            concat_axis=0,
            tiled=True,
        ).reshape(expert_count * capacity, half_width)
        rows = lax.all_gather(arrived, "tensor", axis=1, tiled=True).astype(jnp.float32)
        rms_scale = jnp.sqrt(jnp.mean(rows * rows, axis=1, keepdims=True) + NORM_EPS)
        normed = (rows / rms_scale * gain_row).astype(jnp.bfloat16)
        gate_act = jnp.dot(normed, gate_w, preferred_element_type=jnp.float32)
        up_act = jnp.dot(normed, up_w, preferred_element_type=jnp.float32)
        hidden = (jax.nn.silu(gate_act) * up_act).astype(jnp.bfloat16)
        hidden = lax.all_gather(hidden, "tensor", axis=1, tiled=True)
        partial_out = jnp.dot(hidden, down_w, preferred_element_type=jnp.float32)
        returned = lax.all_to_all(
            partial_out.astype(jnp.bfloat16).reshape(expert_count, capacity, half_width),
            "expert",
            split_axis=0,
            concat_axis=0,
            tiled=True,
        ).astype(jnp.float32)
        expert_out = jnp.sum(returned.reshape(window, 2, capacity, half_width), axis=1)
        moe_sum = lax.dot_general(
            combine_table,
            expert_out.reshape(window * capacity, half_width),
            (((0,), (0,)), ((), ())),
            precision=lax.Precision.HIGHEST,
            preferred_element_type=jnp.float32,
        )
        current = (current.astype(jnp.float32) + moe_sum).astype(jnp.bfloat16)
    return current[None]


def solution(mesh):
    in_specs = (
        P("section", "expert", "tensor"),
        P("section", None),
        P("section", None, ("expert", "tensor")),
        P("section", None, ("expert", "tensor")),
        P("section", ("expert", "tensor"), None),
        P(None, "section", "expert", None),
        P(None, "section", "expert", None),
    )
    out_specs = P("section", "expert", "tensor")
    return jax.shard_map(local, mesh=mesh, in_specs=in_specs, out_specs=out_specs, check_vma=False)
```

```python
import jax
import jax.numpy as jnp
from jax import lax
from jax.sharding import PartitionSpec as P

NORM_EPS = 1e-06


def from_behind(array, by, flip=0):
    sections, experts = lax.axis_size("section"), lax.axis_size("expert")
    pairs = [
        (s * experts + e, (s + by) % sections * experts + (e ^ flip))
        for s in range(sections)
        for e in range(experts)
    ]
    return lax.ppermute(array, ("section", "expert"), pairs)


def slots_of(ids_major, window, capacity):
    tok_count = ids_major.shape[1]
    experts_col = jnp.arange(window, dtype=jnp.int32)[None, :, None]
    member = ids_major[:, None, :] == experts_col
    named = jnp.sum(member.astype(jnp.float32), axis=0)
    row_pos = jnp.arange(tok_count, dtype=jnp.int32)
    strictly = (row_pos[:, None] < row_pos[None, :]).astype(jnp.bfloat16)
    earlier = jnp.dot(named.astype(jnp.bfloat16), strictly, preferred_element_type=jnp.float32)
    slot_col = jnp.arange(capacity, dtype=jnp.float32)[None, :, None]
    filled = named[:, None, :] * (earlier[:, None, :] == slot_col).astype(jnp.float32)
    return filled, member


def dispatch_rows(ids_major, window, capacity):
    filled, _ = slots_of(ids_major, window, capacity)
    return filled.reshape(window * capacity, -1).astype(jnp.bfloat16)


def combine_rows(ids_major, weights_major, window, capacity):
    filled, member = slots_of(ids_major, window, capacity)
    gate_of = jnp.sum(jnp.where(member, weights_major[:, None, :], 0.0), axis=0)
    return (filled * gate_of[:, None, :]).reshape(window * capacity, -1)


def local(activations, norm_gain, w_gate, w_up, w_down, route_ids, route_weights):
    start = activations[0]
    tok_rows, half_width = start.shape
    expert_count = lax.axis_size("expert")
    window = expert_count // 2
    capacity = tok_rows // 16
    slots = expert_count * capacity
    gain_row = norm_gain[0].astype(jnp.float32)
    gate_w = w_gate[0]
    up_w = w_up[0]

    current = from_behind(start, 1)
    routes = jnp.concatenate(
        [route_ids[0, 0].T.astype(jnp.float32), route_weights[0, 0].T], axis=0
    )
    routes_on = from_behind(routes, 1)
    residual = from_behind(start, 2)
    down_w = lax.all_to_all(w_down[0], "tensor", split_axis=1, concat_axis=0, tiled=True)

    def dispatch(tokens, ids):
        table = dispatch_rows(ids, window, capacity)
        twice = jnp.repeat(table.reshape(window, capacity, tok_rows), 2, axis=0)
        outgoing = jnp.dot(
            twice.reshape(slots, tok_rows), tokens, preferred_element_type=jnp.float32
        ).astype(jnp.bfloat16)
        arrived = lax.all_to_all(
            outgoing.reshape(expert_count, capacity, half_width), "expert", 0, 0, tiled=True
        )
        return arrived.reshape(slots, half_width)

    def experts(arrived):
        rows = lax.all_gather(arrived, "tensor", axis=1, tiled=True).astype(jnp.float32)
        rms_scale = jnp.sqrt(jnp.mean(rows * rows, axis=1, keepdims=True) + NORM_EPS)
        normed = (rows / rms_scale * gain_row).astype(jnp.bfloat16)
        gate_act = jnp.dot(normed, gate_w, preferred_element_type=jnp.float32)
        up_act = jnp.dot(normed, up_w, preferred_element_type=jnp.float32)
        hidden = (jax.nn.silu(gate_act) * up_act).astype(jnp.bfloat16)
        hidden = lax.all_gather(hidden, "tensor", axis=1, tiled=True)
        return jnp.dot(hidden, down_w, preferred_element_type=jnp.float32).astype(jnp.bfloat16)

    def combine(tokens, rows, ids, weights):
        moe_sum = lax.dot_general(
            combine_rows(ids, weights, window, capacity),
            rows.astype(jnp.float32),
            (((0,), (0,)), ((), ())),
            precision=lax.Precision.HIGHEST,
            preferred_element_type=jnp.float32,
        )
        return (tokens.astype(jnp.float32) + moe_sum).astype(jnp.bfloat16)

    partial = experts(dispatch(current, route_ids[0, 0].T))
    by_side = partial.reshape(window, 2, capacity, half_width)
    side = lax.axis_index("expert") % 2
    straight = lax.dynamic_index_in_dim(by_side, side, 1, keepdims=False)
    crossed = lax.dynamic_index_in_dim(by_side, 1 - side, 1, keepdims=False)
    halves = from_behind(straight, 1).astype(jnp.float32) + from_behind(crossed, 1, 1).astype(
        jnp.float32
    )
    same_side = [[2 * z + x for z in range(window)] for x in range(2)]
    returned = lax.all_to_all(
        halves.astype(jnp.bfloat16), "expert", 0, 0, tiled=True, axis_index_groups=same_side
    ).reshape(window * capacity, half_width)
    ids_on = routes_on[:6].astype(jnp.int32)
    current = combine(residual, returned, ids_on, routes_on[6:])

    partial = experts(dispatch(current, route_ids[1, 0].T))
    returned = lax.all_to_all(
        partial.reshape(expert_count, capacity, half_width), "expert", 0, 0, tiled=True
    ).astype(jnp.float32)
    expert_out = jnp.sum(returned.reshape(window, 2, capacity, half_width), axis=1)
    current = combine(
        current,
        expert_out.reshape(window * capacity, half_width),
        route_ids[1, 0].T,
        route_weights[1, 0].T,
    )
    return current[None]


def solution(mesh):
    in_specs = (
        P("section", "expert", "tensor"),
        P("section", None),
        P("section", None, ("expert", "tensor")),
        P("section", None, ("expert", "tensor")),
        P("section", ("expert", "tensor"), None),
        P(None, "section", "expert", None),
        P(None, "section", "expert", None),
    )
    out_specs = P("section", "expert", "tensor")
    return jax.shard_map(local, mesh=mesh, in_specs=in_specs, out_specs=out_specs, check_vma=False)
```

```python
import jax
import jax.numpy as jnp
from jax import lax
from jax.sharding import PartitionSpec as P

NORM_EPS = 1e-06


def send(array, by=0, flips=(0, 0)):
    sections, experts, cores = (lax.axis_size(name) for name in ("section", "expert", "tensor"))
    pairs = []
    for s in range(sections):
        for e in range(experts):
            for c in range(cores):
                there = ((s + by) % sections * experts + (e ^ flips[c])) * cores + c
                here = (s * experts + e) * cores + c
                if here != there:
                    pairs.append((here, there))
    return lax.ppermute(array, ("section", "expert", "tensor"), pairs)


def slots_of(ids_major, window, capacity):
    tok_count = ids_major.shape[1]
    experts_col = jnp.arange(window, dtype=jnp.int32)[None, :, None]
    member = ids_major[:, None, :] == experts_col
    named = jnp.sum(member.astype(jnp.float32), axis=0)
    row_pos = jnp.arange(tok_count, dtype=jnp.int32)
    strictly = (row_pos[:, None] < row_pos[None, :]).astype(jnp.bfloat16)
    earlier = jnp.dot(named.astype(jnp.bfloat16), strictly, preferred_element_type=jnp.float32)
    slot_col = jnp.arange(capacity, dtype=jnp.float32)[None, :, None]
    filled = named[:, None, :] * (earlier[:, None, :] == slot_col).astype(jnp.float32)
    return filled, member


def dispatch_rows(ids_major, window, capacity):
    filled, _ = slots_of(ids_major, window, capacity)
    return filled.reshape(window * capacity, -1).astype(jnp.bfloat16)


def combine_rows(ids_major, weights_major, window, capacity):
    filled, member = slots_of(ids_major, window, capacity)
    gate_of = jnp.sum(jnp.where(member, weights_major[:, None, :], 0.0), axis=0)
    return (filled * gate_of[:, None, :]).reshape(window * capacity, -1)


def local(activations, norm_gain, w_gate, w_up, w_down, route_ids, route_weights):
    start = activations[0]
    tok_rows, half_width = start.shape
    expert_count = lax.axis_size("expert")
    window = expert_count // 2
    capacity = tok_rows // 16
    slots = expert_count * capacity
    core = lax.axis_index("tensor")
    side = lax.axis_index("expert") % 2
    gain_row = norm_gain[0].astype(jnp.float32)

    def slot_rows(tokens, twice):
        outgoing = jnp.dot(twice, tokens, preferred_element_type=jnp.float32)
        return outgoing.astype(jnp.bfloat16).reshape(expert_count, capacity, half_width)

    def doubled(table):
        table = jnp.repeat(table.reshape(window, capacity, tok_rows), 2, axis=0)
        return table.reshape(slots, tok_rows)

    def experts(arrived, down_own, down_got):
        rows = lax.all_gather(arrived.reshape(slots, half_width), "tensor", axis=1, tiled=True)
        rows = rows.astype(jnp.float32)
        rms_scale = jnp.sqrt(jnp.mean(rows * rows, axis=1, keepdims=True) + NORM_EPS)
        normed = (rows / rms_scale * gain_row).astype(jnp.bfloat16)
        gate_act = jnp.dot(normed, w_gate[0], preferred_element_type=jnp.float32)
        up_act = jnp.dot(normed, w_up[0], preferred_element_type=jnp.float32)
        hidden = (jax.nn.silu(gate_act) * up_act).astype(jnp.bfloat16)
        hidden = lax.all_gather(hidden, "tensor", axis=0, tiled=False)
        total = jnp.dot(
            lax.dynamic_index_in_dim(hidden, core, 0, keepdims=False),
            down_own,
            preferred_element_type=jnp.float32,
        ) + jnp.dot(
            lax.dynamic_index_in_dim(hidden, 1 - core, 0, keepdims=False),
            down_got,
            preferred_element_type=jnp.float32,
        )
        return total.astype(jnp.bfloat16)

    def combine(tokens, rows, table):
        high = table.astype(jnp.bfloat16)
        low = (table - high.astype(jnp.float32)).astype(jnp.bfloat16)
        dims = (((0,), (0,)), ((), ()))
        moe_sum = lax.dot_general(high, rows, dims, preferred_element_type=jnp.float32)
        moe_sum += lax.dot_general(low, rows, dims, preferred_element_type=jnp.float32)
        return (tokens.astype(jnp.float32) + moe_sum).astype(jnp.bfloat16)

    ids = route_ids[0, 0].T
    outgoing = slot_rows(send(start, 1), doubled(dispatch_rows(ids, window, capacity)))
    routes = jnp.concatenate([ids.astype(jnp.float32), route_weights[0, 0].T], axis=0)
    down_own = lax.dynamic_slice_in_dim(w_down[0], core * half_width, half_width, 1)
    down_sent = lax.dynamic_slice_in_dim(w_down[0], (1 - core) * half_width, half_width, 1)
    outgoing, start, routes, down_sent, down_own = lax.optimization_barrier(
        (outgoing, start, routes, down_sent, down_own)
    )
    arrived = lax.all_to_all(outgoing, "expert", 0, 0, tiled=True)
    residual = send(start, 2)
    routes_on = send(routes, 1)
    down_got = lax.ppermute(down_sent, "tensor", [(0, 1), (1, 0)])
    partial = experts(arrived, down_own, down_got)
    by_side = partial.reshape(window, 2, capacity, half_width)
    straight = lax.dynamic_index_in_dim(by_side, side, 1, keepdims=False)
    crossed = lax.dynamic_index_in_dim(by_side, 1 - side, 1, keepdims=False)
    straight, crossed, residual, routes_on, ids, gates = lax.optimization_barrier(
        (straight, crossed, residual, routes_on, route_ids[1, 0], route_weights[1, 0])
    )
    halves = send(straight, 1).astype(jnp.float32) + send(crossed, 1, (1, 1)).astype(jnp.float32)
    dispatch_1 = doubled(dispatch_rows(ids.T, window, capacity))
    combine_0 = combine_rows(routes_on[:6].astype(jnp.int32), routes_on[6:], window, capacity)
    combine_1 = doubled(combine_rows(ids.T, gates.T, window, capacity))
    halves, combine_0, dispatch_1, combine_1 = lax.optimization_barrier(
        (halves.astype(jnp.bfloat16), combine_0, dispatch_1, combine_1)
    )
    same_side = [[2 * z + x for z in range(window)] for x in range(2)]
    returned = lax.all_to_all(
        halves, "expert", 0, 0, tiled=True, axis_index_groups=same_side
    ).reshape(window * capacity, half_width)
    current = combine(residual, returned, combine_0)

    arrived = lax.all_to_all(slot_rows(current, dispatch_1), "expert", 0, 0, tiled=True)
    partial = experts(arrived, down_own, down_got)
    returned = lax.all_to_all(
        partial.reshape(expert_count, capacity, half_width), "expert", 0, 0, tiled=True
    ).reshape(slots, half_width)
    return combine(current, returned, combine_1)[None]


def solution(mesh):
    in_specs = (
        P("section", "expert", "tensor"),
        P("section", None),
        P("section", None, ("expert", "tensor")),
        P("section", None, ("expert", "tensor")),
        P("section", ("expert", "tensor"), None),
        P(None, "section", "expert", None),
        P(None, "section", "expert", None),
    )
    out_specs = P("section", "expert", "tensor")
    return jax.shard_map(local, mesh=mesh, in_specs=in_specs, out_specs=out_specs, check_vma=False)
```

```python
import jax
import jax.numpy as jnp
from jax import lax
from jax.sharding import PartitionSpec as P

NORM_EPS = 1e-06


def send(array, by=0, flips=(0, 0)):
    sections, experts, cores = (lax.axis_size(name) for name in ("section", "expert", "tensor"))
    pairs = []
    for s in range(sections):
        for e in range(experts):
            for c in range(cores):
                there = ((s + by) % sections * experts + (e ^ flips[c])) * cores + c
                here = (s * experts + e) * cores + c
                if here != there:
                    pairs.append((here, there))
    return lax.ppermute(array, ("section", "expert", "tensor"), pairs)


def round_trip(count):
    return list(range(0, count, 2)) + list(range(count - 1, 0, -2))


def slots_of(ids_major, window, capacity):
    tok_count = ids_major.shape[1]
    experts_col = jnp.array(round_trip(window), dtype=jnp.int32)[None, :, None]
    member = ids_major[:, None, :] == experts_col
    named = jnp.sum(member.astype(jnp.float32), axis=0)
    row_pos = jnp.arange(tok_count, dtype=jnp.int32)
    strictly = (row_pos[:, None] < row_pos[None, :]).astype(jnp.bfloat16)
    earlier = jnp.dot(named.astype(jnp.bfloat16), strictly, preferred_element_type=jnp.float32)
    slot_col = jnp.arange(capacity, dtype=jnp.float32)[None, :, None]
    filled = named[:, None, :] * (earlier[:, None, :] == slot_col).astype(jnp.float32)
    return filled, member


def dispatch_rows(ids_major, window, capacity):
    filled, _ = slots_of(ids_major, window, capacity)
    return filled.reshape(window * capacity, -1).astype(jnp.bfloat16)


def combine_rows(ids_major, weights_major, window, capacity):
    filled, member = slots_of(ids_major, window, capacity)
    gate_of = jnp.sum(jnp.where(member, weights_major[:, None, :], 0.0), axis=0)
    return (filled * gate_of[:, None, :]).reshape(window * capacity, -1).astype(jnp.bfloat16)


def local(activations, norm_gain, w_gate, w_up, w_down, route_ids, route_weights):
    start = activations[0]
    tok_rows, half_width = start.shape
    expert_count = lax.axis_size("expert")
    window = expert_count // 2
    capacity = tok_rows // 16
    slots = expert_count * capacity
    core = lax.axis_index("tensor")
    side = lax.axis_index("expert") % 2
    gain_row = norm_gain[0].astype(jnp.float32)

    def slot_rows(tokens, twice):
        outgoing = jnp.dot(twice, tokens, preferred_element_type=jnp.float32)
        return outgoing.astype(jnp.bfloat16).reshape(expert_count, capacity, half_width)

    def doubled(table):
        return jnp.concatenate([table, table], axis=0)

    same_side = [[2 * z + x for z in round_trip(window)] for x in range(2)]
    both_sides = [same_side[0] + same_side[1]]

    def exchange(chunks, groups):
        return lax.all_to_all(chunks, "expert", 0, 0, tiled=True, axis_index_groups=groups)

    def experts(arrived, down_own, down_got):
        rows = lax.all_gather(arrived.reshape(slots, half_width), "tensor", axis=1, tiled=True)
        rows = rows.astype(jnp.float32)
        rms_scale = jnp.sqrt(jnp.mean(rows * rows, axis=1, keepdims=True) + NORM_EPS)
        normed = (rows / rms_scale * gain_row).astype(jnp.bfloat16)
        gate_act = jnp.dot(normed, w_gate[0], preferred_element_type=jnp.float32)
        up_act = jnp.dot(normed, w_up[0], preferred_element_type=jnp.float32)
        hidden = (jax.nn.silu(gate_act) * up_act).astype(jnp.bfloat16)
        hidden = lax.all_gather(hidden, "tensor", axis=0, tiled=False)
        total = jnp.dot(
            lax.dynamic_index_in_dim(hidden, core, 0, keepdims=False),
            down_own,
            preferred_element_type=jnp.float32,
        ) + jnp.dot(
            lax.dynamic_index_in_dim(hidden, 1 - core, 0, keepdims=False),
            down_got,
            preferred_element_type=jnp.float32,
        )
        return total.astype(jnp.bfloat16)

    def combine(tokens, rows, table):
        dims = (((0,), (0,)), ((), ()))
        moe_sum = lax.dot_general(table, rows, dims, preferred_element_type=jnp.float32)
        return (tokens.astype(jnp.float32) + moe_sum).astype(jnp.bfloat16)

    ids = route_ids[0, 0].T
    outgoing = slot_rows(send(start, 1), doubled(dispatch_rows(ids, window, capacity)))
    routes = jnp.concatenate([ids.astype(jnp.float32), route_weights[0, 0].T], axis=0)
    down_own = lax.dynamic_slice_in_dim(w_down[0], core * half_width, half_width, 1)
    down_sent = lax.dynamic_slice_in_dim(w_down[0], (1 - core) * half_width, half_width, 1)
    outgoing, start, routes, down_sent, down_own = lax.optimization_barrier(
        (outgoing, start, routes, down_sent, down_own)
    )
    arrived = exchange(outgoing, both_sides)
    residual = send(start, 2)
    routes_on = send(routes, 1)
    down_got = lax.ppermute(down_sent, "tensor", [(0, 1), (1, 0)])
    partial = experts(arrived, down_own, down_got)
    by_side = partial.reshape(2, window, capacity, half_width)
    straight = lax.dynamic_index_in_dim(by_side, side, 0, keepdims=False)
    crossed = lax.dynamic_index_in_dim(by_side, 1 - side, 0, keepdims=False)
    straight, crossed, residual, routes_on, ids, gates = lax.optimization_barrier(
        (straight, crossed, residual, routes_on, route_ids[1, 0], route_weights[1, 0])
    )
    halves = send(straight, 1).astype(jnp.float32) + send(crossed, 1, (1, 1)).astype(jnp.float32)
    dispatch_1 = doubled(dispatch_rows(ids.T, window, capacity))
    combine_0 = combine_rows(routes_on[:6].astype(jnp.int32), routes_on[6:], window, capacity)
    combine_1 = doubled(combine_rows(ids.T, gates.T, window, capacity))
    halves, combine_0, dispatch_1, combine_1 = lax.optimization_barrier(
        (halves.astype(jnp.bfloat16), combine_0, dispatch_1, combine_1)
    )
    returned = exchange(halves, same_side).reshape(window * capacity, half_width)
    current = combine(residual, returned, combine_0)

    arrived = exchange(slot_rows(current, dispatch_1), both_sides)
    partial = experts(arrived, down_own, down_got)
    partial = partial.reshape(expert_count, capacity, half_width)
    returned = exchange(partial, both_sides).reshape(slots, half_width)
    return combine(current, returned, combine_1)[None]


def solution(mesh):
    in_specs = (
        P("section", "expert", "tensor"),
        P("section", None),
        P("section", None, ("expert", "tensor")),
        P("section", None, ("expert", "tensor")),
        P("section", ("expert", "tensor"), None),
        P(None, "section", "expert", None),
        P(None, "section", "expert", None),
    )
    out_specs = P("section", "expert", "tensor")
    return jax.shard_map(local, mesh=mesh, in_specs=in_specs, out_specs=out_specs, check_vma=False)
```

```python
import jax
import jax.numpy as jnp
from jax import lax
from jax.sharding import PartitionSpec as P

NORM_EPS = 1e-06


def send(array, by=0, flips=(0, 0)):
    sections, experts, cores = (lax.axis_size(name) for name in ("section", "expert", "tensor"))
    pairs = []
    for s in range(sections):
        for e in range(experts):
            for c in range(cores):
                there = ((s + by) % sections * experts + (e ^ flips[c])) * cores + c
                here = (s * experts + e) * cores + c
                if here != there:
                    pairs.append((here, there))
    return lax.ppermute(array, ("section", "expert", "tensor"), pairs)


def round_trip(count):
    return list(range(0, count, 2)) + list(range(count - 1, 0, -2))


def slots_of(ids_major, window, capacity):
    tok_count = ids_major.shape[1]
    place = lax.broadcasted_iota(jnp.int32, (1, window, 1), 1)
    experts_col = jnp.where(2 * place < window, 2 * place, 2 * window - 1 - 2 * place)
    member = ids_major[:, None, :] == experts_col
    named = jnp.sum(member.astype(jnp.float32), axis=0)
    row_pos = jnp.arange(tok_count, dtype=jnp.int32)
    strictly = (row_pos[:, None] < row_pos[None, :]).astype(jnp.bfloat16)
    earlier = jnp.dot(named.astype(jnp.bfloat16), strictly, preferred_element_type=jnp.float32)
    slot_col = jnp.arange(capacity, dtype=jnp.float32)[None, :, None]
    filled = named[:, None, :] * (earlier[:, None, :] == slot_col).astype(jnp.float32)
    return filled, member


def dispatch_rows(ids_major, window, capacity):
    filled, _ = slots_of(ids_major, window, capacity)
    return filled.reshape(window * capacity, -1).astype(jnp.bfloat16)


def combine_rows(ids_major, weights_major, window, capacity):
    filled, member = slots_of(ids_major, window, capacity)
    gate_of = jnp.sum(jnp.where(member, weights_major[:, None, :], 0.0), axis=0)
    return (filled * gate_of[:, None, :]).reshape(window * capacity, -1).astype(jnp.bfloat16)


def local(activations, norm_gain, w_gate, w_up, w_down, route_ids, route_weights):
    start = activations[0]
    tok_rows, half_width = start.shape
    expert_count = lax.axis_size("expert")
    window = expert_count // 2
    capacity = tok_rows // 16
    slots = expert_count * capacity
    core = lax.axis_index("tensor")
    side = lax.axis_index("expert") % 2

    def slot_rows(tokens, twice):
        outgoing = jnp.dot(twice, tokens, preferred_element_type=jnp.float32)
        return outgoing.astype(jnp.bfloat16).reshape(expert_count, capacity, half_width)

    def doubled(table):
        return jnp.concatenate([table, table], axis=0)

    same_side = [[2 * z + x for z in round_trip(window)] for x in range(2)]
    both_sides = [same_side[0] + same_side[1]]

    def exchange(chunks, groups):
        return lax.all_to_all(chunks, "expert", 0, 0, tiled=True, axis_index_groups=groups)

    def experts(arrived, down_own, down_got):
        rows = lax.all_gather(arrived.reshape(slots, half_width), "tensor", axis=1, tiled=True)
        rows = rows.astype(jnp.float32)
        rms_scale = jnp.sqrt(jnp.mean(rows * rows, axis=1, keepdims=True) + NORM_EPS)
        normed = (rows / rms_scale * gain_row).astype(jnp.bfloat16)
        gate_act = jnp.dot(normed, w_gate[0], preferred_element_type=jnp.float32)
        up_act = jnp.dot(normed, w_up[0], preferred_element_type=jnp.float32)
        hidden = (jax.nn.silu(gate_act) * up_act).astype(jnp.bfloat16)
        hidden = lax.all_gather(hidden, "tensor", axis=0, tiled=False)
        total = jnp.dot(
            lax.dynamic_index_in_dim(hidden, core, 0, keepdims=False),
            down_own,
            preferred_element_type=jnp.float32,
        ) + jnp.dot(
            lax.dynamic_index_in_dim(hidden, 1 - core, 0, keepdims=False),
            down_got,
            preferred_element_type=jnp.float32,
        )
        return total.astype(jnp.bfloat16)

    def combine(tokens, rows, table):
        dims = (((0,), (0,)), ((), ()))
        moe_sum = lax.dot_general(table, rows, dims, preferred_element_type=jnp.float32)
        return (tokens.astype(jnp.float32) + moe_sum).astype(jnp.bfloat16)

    ids = route_ids[0, 0].T
    shifted = send(start, 1, (0, 1))
    pairs = [[2 * z, 2 * z + 1] for z in range(window)]
    both_ids = lax.all_gather(ids, "expert", axis_index_groups=pairs)
    ids_here = jnp.where(side == core, both_ids[0], both_ids[1])
    outgoing = slot_rows(shifted, doubled(dispatch_rows(ids_here, window, capacity)))
    down_sent = lax.dynamic_slice_in_dim(w_down[0], (1 - core) * half_width, half_width, 1)
    outgoing, start, gates, down_sent, down_all, gain = lax.optimization_barrier(
        (outgoing, start, route_weights, down_sent, w_down[0], norm_gain)
    )
    gain_row = gain.astype(jnp.float32)
    down_own = lax.dynamic_slice_in_dim(down_all, core * half_width, half_width, 1)
    routes = jnp.concatenate([ids.astype(jnp.float32), gates[0, 0].T], axis=0)
    orders = [
        [2 * e for e in same_side[0] + same_side[1]],
        [2 * e + 1 for e in same_side[1] + same_side[0]],
    ]
    arrived = lax.all_to_all(
        outgoing, ("expert", "tensor"), 0, 0, tiled=True, axis_index_groups=orders
    )
    residual = send(start, 2)
    routes_on = send(routes, 1)
    down_got = lax.ppermute(down_sent, "tensor", [(0, 1), (1, 0)])
    partial = experts(arrived, down_own, down_got)
    by_side = partial.reshape(2, window, capacity, half_width)
    straight = lax.dynamic_index_in_dim(by_side, side, 0, keepdims=False)
    crossed = lax.dynamic_index_in_dim(by_side, 1 - side, 0, keepdims=False)
    straight, crossed, residual, routes_on, ids, gates = lax.optimization_barrier(
        (straight, crossed, residual, routes_on, route_ids[1, 0], gates[1, 0])
    )
    halves = send(straight, 1).astype(jnp.float32) + send(crossed, 1, (1, 1)).astype(jnp.float32)
    dispatch_1 = doubled(dispatch_rows(ids.T, window, capacity))
    combine_0 = combine_rows(routes_on[:6].astype(jnp.int32), routes_on[6:], window, capacity)
    combine_1 = doubled(combine_rows(ids.T, gates.T, window, capacity))
    halves, combine_0, dispatch_1, combine_1 = lax.optimization_barrier(
        (halves.astype(jnp.bfloat16), combine_0, dispatch_1, combine_1)
    )
    returned = exchange(halves, same_side).reshape(window * capacity, half_width)
    current = combine(residual, returned, combine_0)

    arrived = exchange(slot_rows(current, dispatch_1), both_sides)
    partial = experts(arrived, down_own, down_got)
    partial = partial.reshape(expert_count, capacity, half_width)
    returned = exchange(partial, both_sides).reshape(slots, half_width)
    return combine(current, returned, combine_1)[None]


def solution(mesh):
    in_specs = (
        P("section", "expert", "tensor"),
        P("section", None),
        P("section", None, ("expert", "tensor")),
        P("section", None, ("expert", "tensor")),
        P("section", ("expert", "tensor"), None),
        P(None, "section", "expert", None),
        P(None, "section", "expert", None),
    )
    out_specs = P("section", "expert", "tensor")
    return jax.shard_map(local, mesh=mesh, in_specs=in_specs, out_specs=out_specs, check_vma=False)
```

```python
import jax
import jax.numpy as jnp
from jax import lax
from jax.sharding import PartitionSpec as P

NORM_EPS = 1e-06


def send(array, by=0, flips=(0, 0)):
    sections, experts, cores = (lax.axis_size(name) for name in ("section", "expert", "tensor"))
    pairs = []
    for s in range(sections):
        for e in range(experts):
            for c in range(cores):
                there = ((s + by) % sections * experts + (e ^ flips[c])) * cores + c
                here = (s * experts + e) * cores + c
                if here != there:
                    pairs.append((here, there))
    return lax.ppermute(array, ("section", "expert", "tensor"), pairs)


def round_trip(count):
    return [-2 * i % count for i in range(count // 2)] + list(range(1, count, 2))


def slots_of(ids_major, window, capacity):
    tok_count = ids_major.shape[1]
    place = lax.broadcasted_iota(jnp.int32, (1, window, 1), 1)
    experts_col = jnp.where(2 * place < window, window - 2 * place, 2 * place - window + 1)
    experts_col = jnp.where(place == 0, 0, experts_col)
    member = ids_major[:, None, :] == experts_col
    named = jnp.sum(member.astype(jnp.float32), axis=0)
    row_pos = jnp.arange(tok_count, dtype=jnp.int32)
    strictly = (row_pos[:, None] < row_pos[None, :]).astype(jnp.bfloat16)
    earlier = jnp.dot(named.astype(jnp.bfloat16), strictly, preferred_element_type=jnp.float32)
    slot_col = jnp.arange(capacity, dtype=jnp.float32)[None, :, None]
    filled = named[:, None, :] * (earlier[:, None, :] == slot_col).astype(jnp.float32)
    return filled, member


def dispatch_rows(ids_major, window, capacity):
    filled, _ = slots_of(ids_major, window, capacity)
    return filled.reshape(window * capacity, -1).astype(jnp.bfloat16)


def combine_rows(ids_major, weights_major, window, capacity):
    filled, member = slots_of(ids_major, window, capacity)
    gate_of = jnp.sum(jnp.where(member, weights_major[:, None, :], 0.0), axis=0)
    return (filled * gate_of[:, None, :]).reshape(window * capacity, -1).astype(jnp.bfloat16)


def local(activations, norm_gain, w_gate, w_up, w_down, route_ids, route_weights):
    start = activations[0]
    tok_rows, half_width = start.shape
    expert_count = lax.axis_size("expert")
    window = expert_count // 2
    capacity = tok_rows // 16
    slots = expert_count * capacity
    core = lax.axis_index("tensor")
    side = lax.axis_index("expert") % 2

    def slot_rows(tokens, twice):
        outgoing = jnp.dot(twice, tokens, preferred_element_type=jnp.float32)
        return outgoing.astype(jnp.bfloat16).reshape(expert_count, capacity, half_width)

    def doubled(table):
        return jnp.concatenate([table, table], axis=0)

    same_side = [[2 * z + x for z in round_trip(window)] for x in range(2)]
    both_sides = [same_side[0] + same_side[1]]

    def exchange(chunks, groups):
        return lax.all_to_all(chunks, "expert", 0, 0, tiled=True, axis_index_groups=groups)

    def experts(arrived, down_own, down_got):
        rows = lax.all_gather(arrived.reshape(slots, half_width), "tensor", axis=1, tiled=True)
        rows = rows.astype(jnp.float32)
        rms_scale = jnp.sqrt(jnp.mean(rows * rows, axis=1, keepdims=True) + NORM_EPS)
        normed = (rows / rms_scale * gain_row).astype(jnp.bfloat16)
        gate_act = jnp.dot(normed, w_gate[0], preferred_element_type=jnp.float32)
        up_act = jnp.dot(normed, w_up[0], preferred_element_type=jnp.float32)
        hidden = (jax.nn.silu(gate_act) * up_act).astype(jnp.bfloat16)
        hidden = lax.all_gather(hidden, "tensor", axis=0, tiled=False)
        total = jnp.dot(
            lax.dynamic_index_in_dim(hidden, core, 0, keepdims=False),
            down_own,
            preferred_element_type=jnp.float32,
        ) + jnp.dot(
            lax.dynamic_index_in_dim(hidden, 1 - core, 0, keepdims=False),
            down_got,
            preferred_element_type=jnp.float32,
        )
        return total.astype(jnp.bfloat16)

    def combine(tokens, rows, table):
        dims = (((0,), (0,)), ((), ()))
        moe_sum = lax.dot_general(table, rows, dims, preferred_element_type=jnp.float32)
        return (tokens.astype(jnp.float32) + moe_sum).astype(jnp.bfloat16)

    ids = route_ids[0, 0].T
    shifted = send(start, 1, (0, 1))
    pairs = [[2 * z, 2 * z + 1] for z in range(window)]
    both_ids = lax.all_gather(ids, "expert", axis_index_groups=pairs)
    ids_here = jnp.where(side == core, both_ids[0], both_ids[1])
    outgoing = slot_rows(shifted, doubled(dispatch_rows(ids_here, window, capacity)))
    down_sent = lax.dynamic_slice_in_dim(w_down[0], (1 - core) * half_width, half_width, 1)
    outgoing, start, gates, down_sent, down_all, gain = lax.optimization_barrier(
        (outgoing, start, route_weights, down_sent, w_down[0], norm_gain)
    )
    gain_row = gain.astype(jnp.float32)
    down_own = lax.dynamic_slice_in_dim(down_all, core * half_width, half_width, 1)
    routes = jnp.concatenate([ids.astype(jnp.float32), gates[0, 0].T], axis=0)
    orders = [
        [2 * e for e in same_side[0] + same_side[1]],
        [2 * e + 1 for e in same_side[1] + same_side[0]],
    ]
    arrived = lax.all_to_all(
        outgoing, ("expert", "tensor"), 0, 0, tiled=True, axis_index_groups=orders
    )
    residual = send(start, 2)
    routes_on = send(routes, 1)
    down_got = lax.ppermute(down_sent, "tensor", [(0, 1), (1, 0)])
    partial = experts(arrived, down_own, down_got)
    by_side = partial.reshape(2, window, capacity, half_width)
    straight = lax.dynamic_index_in_dim(by_side, side, 0, keepdims=False)
    crossed = lax.dynamic_index_in_dim(by_side, 1 - side, 0, keepdims=False)
    straight, crossed, residual, routes_on, ids, gates = lax.optimization_barrier(
        (straight, crossed, residual, routes_on, route_ids[1, 0], gates[1, 0])
    )
    halves = send(straight, 1).astype(jnp.float32) + send(crossed, 1, (1, 1)).astype(jnp.float32)
    dispatch_1 = doubled(dispatch_rows(ids.T, window, capacity))
    combine_0 = combine_rows(routes_on[:6].astype(jnp.int32), routes_on[6:], window, capacity)
    combine_1 = doubled(combine_rows(ids.T, gates.T, window, capacity))
    halves, combine_0, dispatch_1, combine_1 = lax.optimization_barrier(
        (halves.astype(jnp.bfloat16), combine_0, dispatch_1, combine_1)
    )
    returned = exchange(halves, same_side).reshape(window * capacity, half_width)
    current = combine(residual, returned, combine_0)

    arrived = exchange(slot_rows(current, dispatch_1), both_sides)
    partial = experts(arrived, down_own, down_got)
    partial = partial.reshape(expert_count, capacity, half_width)
    returned = exchange(partial, both_sides).reshape(slots, half_width)
    return combine(current, returned, combine_1)[None]


def solution(mesh):
    in_specs = (
        P("section", "expert", "tensor"),
        P("section", None),
        P("section", None, ("expert", "tensor")),
        P("section", None, ("expert", "tensor")),
        P("section", ("expert", "tensor"), None),
        P(None, "section", "expert", None),
        P(None, "section", "expert", None),
    )
    out_specs = P("section", "expert", "tensor")
    return jax.shard_map(local, mesh=mesh, in_specs=in_specs, out_specs=out_specs, check_vma=False)
```

```python
import jax
import jax.numpy as jnp
from jax import lax
from jax.sharding import PartitionSpec as P

NORM_EPS = 1e-06


def send(array, by=0, flips=(0, 0)):
    sections, experts, cores = (lax.axis_size(name) for name in ("section", "expert", "tensor"))
    pairs = []
    for s in range(sections):
        for e in range(experts):
            for c in range(cores):
                there = ((s + by) % sections * experts + (e ^ flips[c])) * cores + c
                here = (s * experts + e) * cores + c
                if here != there:
                    pairs.append((here, there))
    return lax.ppermute(array, ("section", "expert", "tensor"), pairs)


def round_trip(count):
    return [-2 * i % count for i in range(count // 2)] + list(range(1, count, 2))


def slots_of(ids_major, window, capacity):
    tok_count = ids_major.shape[1]
    place = lax.broadcasted_iota(jnp.int32, (1, window, 1), 1)
    experts_col = jnp.where(2 * place < window, window - 2 * place, 2 * place - window + 1)
    experts_col = jnp.where(place == 0, 0, experts_col)
    member = ids_major[:, None, :] == experts_col
    named = jnp.sum(member.astype(jnp.float32), axis=0)
    row_pos = jnp.arange(tok_count, dtype=jnp.int32)
    strictly = (row_pos[:, None] < row_pos[None, :]).astype(jnp.bfloat16)
    earlier = jnp.dot(named.astype(jnp.bfloat16), strictly, preferred_element_type=jnp.float32)
    slot_col = jnp.arange(capacity, dtype=jnp.float32)[None, :, None]
    filled = named[:, None, :] * (earlier[:, None, :] == slot_col).astype(jnp.float32)
    return filled, member


def dispatch_rows(ids_major, window, capacity):
    filled, _ = slots_of(ids_major, window, capacity)
    return filled.reshape(window * capacity, -1).astype(jnp.bfloat16)


def combine_rows(ids_major, weights_major, window, capacity):
    filled, member = slots_of(ids_major, window, capacity)
    gate_of = jnp.sum(jnp.where(member, weights_major[:, None, :], 0.0), axis=0)
    return (filled * gate_of[:, None, :]).reshape(window * capacity, -1).astype(jnp.bfloat16)


def local(activations, norm_gain, w_gate, w_up, w_down, route_ids, route_weights):
    start = activations[0]
    tok_rows, half_width = start.shape
    expert_count = lax.axis_size("expert")
    window = expert_count // 2
    capacity = tok_rows // 16
    slots = expert_count * capacity
    core = lax.axis_index("tensor")
    side = lax.axis_index("expert") % 2

    def slot_rows(tokens, twice):
        outgoing = jnp.dot(twice, tokens, preferred_element_type=jnp.float32)
        return outgoing.astype(jnp.bfloat16).reshape(expert_count, capacity, half_width)

    def doubled(table):
        return jnp.concatenate([table, table], axis=0)

    same_side = [[2 * z + x for z in round_trip(window)] for x in range(2)]
    both_sides = [same_side[0] + same_side[1]]

    def exchange(chunks, groups):
        return lax.all_to_all(chunks, "expert", 0, 0, tiled=True, axis_index_groups=groups)

    def experts(arrived, down_own, down_got):
        rows = lax.all_gather(arrived.reshape(slots, half_width), "tensor", axis=1, tiled=True)
        rows = rows.astype(jnp.float32)
        rms_scale = jnp.sqrt(jnp.mean(rows * rows, axis=1, keepdims=True) + NORM_EPS)
        normed = (rows / rms_scale * gain_row).astype(jnp.bfloat16)
        gate_act = jnp.dot(normed, w_gate[0], preferred_element_type=jnp.float32)
        up_act = jnp.dot(normed, w_up[0], preferred_element_type=jnp.float32)
        hidden = (jax.nn.silu(gate_act) * up_act).astype(jnp.bfloat16)
        hidden = lax.all_gather(hidden, "tensor", axis=0, tiled=False)
        total = jnp.dot(
            lax.dynamic_index_in_dim(hidden, core, 0, keepdims=False),
            down_own,
            preferred_element_type=jnp.float32,
        ) + jnp.dot(
            lax.dynamic_index_in_dim(hidden, 1 - core, 0, keepdims=False),
            down_got,
            preferred_element_type=jnp.float32,
        )
        return total.astype(jnp.bfloat16)

    def combine(tokens, rows, table):
        dims = (((0,), (0,)), ((), ()))
        moe_sum = lax.dot_general(table, rows, dims, preferred_element_type=jnp.float32)
        return (tokens.astype(jnp.float32) + moe_sum).astype(jnp.bfloat16)

    shifted = send(start, 1, (0, 1))
    pairs = [[2 * z, 2 * z + 1] for z in range(window)]
    both_ids = lax.all_gather(route_ids, "expert", axis_index_groups=pairs)
    ids_here = jnp.where(side == core, both_ids[0, 0, 0].T, both_ids[1, 0, 0].T)
    outgoing = slot_rows(shifted, doubled(dispatch_rows(ids_here, window, capacity)))
    down_sent = lax.dynamic_slice_in_dim(w_down[0], (1 - core) * half_width, half_width, 1)
    outgoing, start, ids, gates, down_sent, down_all, gain = lax.optimization_barrier(
        (outgoing, start, route_ids, route_weights, down_sent, w_down[0], norm_gain)
    )
    gain_row = gain.astype(jnp.float32)
    down_own = lax.dynamic_slice_in_dim(down_all, core * half_width, half_width, 1)
    routes = jnp.concatenate([ids[0, 0].T.astype(jnp.float32), gates[0, 0].T], axis=0)
    orders = [
        [2 * e for e in same_side[0] + same_side[1]],
        [2 * e + 1 for e in same_side[1] + same_side[0]],
    ]
    arrived = lax.all_to_all(
        outgoing, ("expert", "tensor"), 0, 0, tiled=True, axis_index_groups=orders
    )
    residual = send(start, 2)
    routes_on = send(routes, 1)
    down_got = lax.ppermute(down_sent, "tensor", [(0, 1), (1, 0)])
    partial = experts(arrived, down_own, down_got)
    by_side = partial.reshape(2, window, capacity, half_width)
    straight = lax.dynamic_index_in_dim(by_side, side, 0, keepdims=False)
    crossed = lax.dynamic_index_in_dim(by_side, 1 - side, 0, keepdims=False)
    straight, crossed, residual, routes_on, ids, gates = lax.optimization_barrier(
        (straight, crossed, residual, routes_on, ids[1, 0], gates[1, 0])
    )
    halves = send(straight, 1).astype(jnp.float32) + send(crossed, 1, (1, 1)).astype(jnp.float32)
    dispatch_1 = doubled(dispatch_rows(ids.T, window, capacity))
    combine_0 = combine_rows(routes_on[:6].astype(jnp.int32), routes_on[6:], window, capacity)
    combine_1 = doubled(combine_rows(ids.T, gates.T, window, capacity))
    halves, combine_0, dispatch_1, combine_1 = lax.optimization_barrier(
        (halves.astype(jnp.bfloat16), combine_0, dispatch_1, combine_1)
    )
    returned = exchange(halves, same_side).reshape(window * capacity, half_width)
    current = combine(residual, returned, combine_0)

    arrived = exchange(slot_rows(current, dispatch_1), both_sides)
    partial = experts(arrived, down_own, down_got)
    partial = partial.reshape(expert_count, capacity, half_width)
    returned = exchange(partial, both_sides).reshape(slots, half_width)
    return combine(current, returned, combine_1)[None]


def solution(mesh):
    in_specs = (
        P("section", "expert", "tensor"),
        P("section", None),
        P("section", None, ("expert", "tensor")),
        P("section", None, ("expert", "tensor")),
        P("section", ("expert", "tensor"), None),
        P(None, "section", "expert", None),
        P(None, "section", "expert", None),
    )
    out_specs = P("section", "expert", "tensor")
    return jax.shard_map(local, mesh=mesh, in_specs=in_specs, out_specs=out_specs, check_vma=False)
```

```python
import jax
import jax.numpy as jnp
from jax import lax
from jax.sharding import PartitionSpec as P

NORM_EPS = 1e-06


def send(array, by=0, flips=(0, 0)):
    sections, experts, cores = (lax.axis_size(name) for name in ("section", "expert", "tensor"))
    pairs = []
    for s in range(sections):
        for e in range(experts):
            for c in range(cores):
                there = ((s + by) % sections * experts + (e ^ flips[c])) * cores + c
                here = (s * experts + e) * cores + c
                if here != there:
                    pairs.append((here, there))
    return lax.ppermute(array, ("section", "expert", "tensor"), pairs)


def round_trip(count):
    return [-2 * i % count for i in range(count // 2)] + list(range(1, count, 2))


def slots_of(ids_major, window, capacity):
    tok_count = ids_major.shape[1]
    place = lax.broadcasted_iota(jnp.int32, (1, window, 1), 1)
    experts_col = jnp.where(2 * place < window, window - 2 * place, 2 * place - window + 1)
    experts_col = jnp.where(place == 0, 0, experts_col)
    member = ids_major[:, None, :] == experts_col
    named = jnp.sum(member.astype(jnp.float32), axis=0)
    row_pos = jnp.arange(tok_count, dtype=jnp.int32)
    strictly = (row_pos[:, None] < row_pos[None, :]).astype(jnp.bfloat16)
    earlier = jnp.dot(named.astype(jnp.bfloat16), strictly, preferred_element_type=jnp.float32)
    slot_col = jnp.arange(capacity, dtype=jnp.float32)[None, :, None]
    filled = named[:, None, :] * (earlier[:, None, :] == slot_col).astype(jnp.float32)
    return filled, member


def dispatch_rows(ids_major, window, capacity):
    filled, _ = slots_of(ids_major, window, capacity)
    return filled.reshape(window * capacity, -1).astype(jnp.bfloat16)


def combine_rows(ids_major, weights_major, window, capacity):
    filled, member = slots_of(ids_major, window, capacity)
    gate_of = jnp.sum(jnp.where(member, weights_major[:, None, :], 0.0), axis=0)
    return (filled * gate_of[:, None, :]).reshape(window * capacity, -1).astype(jnp.bfloat16)


def local(activations, norm_gain, w_gate, w_up, w_down, route_ids, route_weights):
    start = activations[0]
    tok_rows, half_width = start.shape
    expert_count = lax.axis_size("expert")
    window = expert_count // 2
    capacity = tok_rows // 16
    slots = expert_count * capacity
    core = lax.axis_index("tensor")
    side = lax.axis_index("expert") % 2

    def slot_rows(tokens, twice):
        outgoing = jnp.dot(twice, tokens, preferred_element_type=jnp.float32)
        return outgoing.astype(jnp.bfloat16).reshape(expert_count, capacity, half_width)

    def doubled(table):
        return jnp.concatenate([table, table], axis=0)

    same_side = [[2 * z + x for z in round_trip(window)] for x in range(2)]
    both_sides = [same_side[0] + same_side[1]]

    def exchange(chunks, groups):
        return lax.all_to_all(chunks, "expert", 0, 0, tiled=True, axis_index_groups=groups)

    def experts(arrived, down_own, down_got):
        rows = lax.all_gather(arrived.reshape(slots, half_width), "tensor", axis=1, tiled=True)
        rows = rows.astype(jnp.float32)
        scale = 1.0 / jnp.sqrt(jnp.mean(rows * rows, axis=1, keepdims=True) + NORM_EPS)
        normed = (rows * scale * gain_row).astype(jnp.bfloat16)
        gate_act = jnp.dot(normed, w_gate[0], preferred_element_type=jnp.float32)
        up_act = jnp.dot(normed, w_up[0], preferred_element_type=jnp.float32)
        hidden = (jax.nn.silu(gate_act) * up_act).astype(jnp.bfloat16)
        hidden = lax.all_gather(hidden, "tensor", axis=0, tiled=False)
        total = jnp.dot(
            lax.dynamic_index_in_dim(hidden, core, 0, keepdims=False),
            down_own,
            preferred_element_type=jnp.float32,
        ) + jnp.dot(
            lax.dynamic_index_in_dim(hidden, 1 - core, 0, keepdims=False),
            down_got,
            preferred_element_type=jnp.float32,
        )
        return total.astype(jnp.bfloat16)

    def combine(tokens, rows, table):
        dims = (((0,), (0,)), ((), ()))
        moe_sum = lax.dot_general(table, rows, dims, preferred_element_type=jnp.float32)
        return (tokens.astype(jnp.float32) + moe_sum).astype(jnp.bfloat16)

    shifted = send(start, 1, (0, 1))
    pairs = [[2 * z, 2 * z + 1] for z in range(window)]
    both_ids = lax.all_gather(route_ids, "expert", axis_index_groups=pairs)
    ids_here = jnp.where(side == core, both_ids[0, 0, 0].T, both_ids[1, 0, 0].T)
    outgoing = slot_rows(shifted, doubled(dispatch_rows(ids_here, window, capacity)))
    down_sent = lax.dynamic_slice_in_dim(w_down[0], (1 - core) * half_width, half_width, 1)
    outgoing, start, ids, gates, down_sent, down_all, gain = lax.optimization_barrier(
        (outgoing, start, route_ids, route_weights, down_sent, w_down[0], norm_gain)
    )
    gain_row = gain.astype(jnp.float32)
    down_own = lax.dynamic_slice_in_dim(down_all, core * half_width, half_width, 1)
    routes = jnp.concatenate([ids[0, 0].T.astype(jnp.float32), gates[0, 0].T], axis=0)
    orders = [
        [2 * e for e in same_side[0] + same_side[1]],
        [2 * e + 1 for e in same_side[1] + same_side[0]],
    ]
    arrived = lax.all_to_all(
        outgoing, ("expert", "tensor"), 0, 0, tiled=True, axis_index_groups=orders
    )
    residual = send(start, 2)
    routes_on = send(routes, 1)
    down_got = lax.ppermute(down_sent, "tensor", [(0, 1), (1, 0)])
    partial = experts(arrived, down_own, down_got)
    by_side = partial.reshape(2, window, capacity, half_width)
    straight = lax.dynamic_index_in_dim(by_side, side, 0, keepdims=False)
    crossed = lax.dynamic_index_in_dim(by_side, 1 - side, 0, keepdims=False)
    straight, crossed, residual, routes_on, ids, gates = lax.optimization_barrier(
        (straight, crossed, residual, routes_on, ids[1, 0], gates[1, 0])
    )
    halves = send(straight, 1).astype(jnp.float32) + send(crossed, 1, (1, 1)).astype(jnp.float32)
    dispatch_1 = doubled(dispatch_rows(ids.T, window, capacity))
    combine_0 = combine_rows(routes_on[:6].astype(jnp.int32), routes_on[6:], window, capacity)
    combine_1 = doubled(combine_rows(ids.T, gates.T, window, capacity))
    halves, combine_0, dispatch_1, combine_1 = lax.optimization_barrier(
        (halves.astype(jnp.bfloat16), combine_0, dispatch_1, combine_1)
    )
    returned = exchange(halves, same_side).reshape(window * capacity, half_width)
    current = combine(residual, returned, combine_0)

    arrived = exchange(slot_rows(current, dispatch_1), both_sides)
    partial = experts(arrived, down_own, down_got)
    partial = partial.reshape(expert_count, capacity, half_width)
    returned = exchange(partial, both_sides).reshape(slots, half_width)
    return combine(current, returned, combine_1)[None]


def solution(mesh):
    in_specs = (
        P("section", "expert", "tensor"),
        P("section", None),
        P("section", None, ("expert", "tensor")),
        P("section", None, ("expert", "tensor")),
        P("section", ("expert", "tensor"), None),
        P(None, "section", "expert", None),
        P(None, "section", "expert", None),
    )
    out_specs = P("section", "expert", "tensor")
    return jax.shard_map(local, mesh=mesh, in_specs=in_specs, out_specs=out_specs, check_vma=False)
```
